32 devices in a mesh: dp: 4 (over y, x), expert: 8 (over z, core).
Axes of the slice: x: 2, y: 2, z: 4, core: 2. Of those that a mesh axis runs over, the one named last changes fastest.
Arguments:
- activations: bfloat16 [1024, 7168], P('expert'), may hold values from -0.25 to 0.25
- expert_ids: int32 [1024, 8], P('expert'), may hold values from 0 to 31, all different within a row; in each aligned block of 128 rows (0 to 127, 128 to 255, ...) at most 48 rows name the same one
- gate_weights: float32 [1024, 8], P('expert'), may hold values from 0.2 to 1
- slot_grads: bfloat16 [32, 384, 1024], P('expert', 'dp'), may hold values from -6 to 6
- expert_weights: bfloat16 [32, 7168, 1024], P('expert', 'dp'), may hold values from -0.1875 to 0.1875
- shared_grads: bfloat16 [1024, 1024], P('expert'), may hold values from -6 to 6
- shared_weight: bfloat16 [7168, 1024], P('dp'), may hold values from -0.1875 to 0.1875
Outputs:
- rotation_grad: float32 [7168, 7168], P('expert', 'dp')
The draws below stay inside these ranges and needn't reach their ends.
Inputs may be any that keep to these rules, and one draw needn't show every extreme that they name: `expert_ids`: each token names 8 different experts. In each aligned block of 128 tokens no expert is named by more than 48 tokens, a bound that some block reaches.
All inputs are finite; a program needn't handle non-finite values.
Results may differ from the reference program's by a relative error of at most 0.0075.
Values may be sent and summed in bfloat16 or wider, within the bound.
A program may use at most 192 MiB of HBM per device.

```python
import math
import jax
import jax.numpy as jnp
import numpy as np
from jax import lax

D = 7168
FF = 1024
TOP = 8
TOK_J = 128
EXPERTS = 32
TOKENS = 1024
SLOTS = 384
CAP = 48
N_EXPERT = 8


def spiked(array, key, source, target, blocks, factor):
    def block_of(dim):
        return (jnp.arange(array.shape[dim]) // (array.shape[dim] // blocks)).reshape((-1,) + (1,) * (array.ndim - 1 - dim))

    one_side = jax.random.permutation(key, blocks)[block_of(target)]
    other_side = (block_of(target) + blocks // 2) % blocks
    return jnp.where((block_of(source) == one_side) | (block_of(source) == other_side), factor * array, array)


def steps_of(rng, extent, split, smallest, high):
    def one(axis_at, parts):
        draws = jax.random.uniform(jax.random.fold_in(jax.random.fold_in(rng, 6), axis_at), (parts,), jnp.float32, smallest / len(split), high / len(split))
        return jnp.repeat(jnp.exp(draws), extent[axis_at] // parts).reshape((-1,) + (1,) * (len(extent) - axis_at - 1))

    level = one(*split[0])
    for cut in split[1:]:
        level = level * one(*cut)
    return level


def shared_out(stream_key, own, number, rows, number_of, top, limit, slope):
    order = jax.random.permutation(stream_key, number_of)
    crowded, common = load_shares(number_of, rows * top, limit, slope, True), load_shares(number_of, rows * top, limit, slope, False)
    places = jnp.arange(number_of)

    def named(sizes, turn):
        used = int((sizes > 0).sum())
        fixed = max(1, used // 4)
        passed = fixed + (places - fixed + turn * (used - fixed)) % max(1, number_of - fixed)
        return jnp.zeros((number_of,), jnp.int32).at[order[jnp.where(places < fixed, places, passed)]].set(jnp.asarray(sizes, jnp.int32))

    sizes = jnp.where(number % 4 == 0, named(crowded, number // 4), named(common, number - number // 4 - 1))
    mixed = jax.random.permutation(jax.random.fold_in(own, 3), number_of)
    donor, taker = mixed[0:number_of // 2 * 2:2], mixed[1:number_of // 2 * 2:2]
    room = jnp.minimum(sizes[donor] - 1, limit - sizes[taker]) // 2
    room = jnp.where((donor == order[0]) | (taker == order[0]) | (sizes[taker] == 0), 0, jnp.maximum(room, 0))
    passed = jax.random.randint(jax.random.fold_in(own, 4), (number_of // 2,), 0, 1 << 20) % (room + 1)
    sizes = sizes.at[donor].add(-passed).at[taker].add(passed)
    items = jnp.searchsorted(jnp.cumsum(sizes), jnp.arange(rows * top), side="right").astype(jnp.int32)
    grid = items.reshape(top, rows).T
    grid = grid[jax.random.permutation(jax.random.fold_in(own, 1), rows)]
    turn = jax.random.randint(jax.random.fold_in(own, 2), (rows, 1), 0, top)
    return jnp.take_along_axis(grid, (jnp.arange(top)[None, :] + turn) % top, axis=1)


def load_shares(number_of, total, limit, slope, full):
    loads = [(1 << 20) // math.isqrt(rank ** slope) + 1 for rank in range(1, number_of + 1)]
    largest = limit if full else min(limit, max(-(-total // number_of), total * loads[0] // sum(loads)))
    least = 1 if total - largest >= number_of - 1 else 0
    counts, surplus = [largest] + [least] * (number_of - 1), total - largest - least * (number_of - 1)
    while surplus > 0:
        movable = [i for i in range(1, number_of) if counts[i] < largest] or [i for i in range(1, number_of) if counts[i] < limit]
        mass, left = sum([loads[i] for i in movable]), surplus
        for i in movable:
            addition = min(limit - counts[i], max(1, left * loads[i] // mass), surplus)
            counts[i] = counts[i] + addition
            surplus = surplus - addition
    return np.array(counts)


def gaussian(key, shape, scale, reach, cuts=(), held_as=jnp.bfloat16):
    drawn = jax.random.normal(key, shape, jnp.float32) * scale
    if len(cuts) > 0:
        drawn = steps_of(key, shape, cuts, -0.22, 0.18) * drawn
    return jnp.clip(drawn, min=-reach, max=reach).astype(held_as)


def bell_draw_with(rng, dims, scale, reach, shards, heavy, kind=jnp.bfloat16):
    values = scale * jax.random.normal(rng, dims, jnp.float32)
    if shards:
        values = values * steps_of(rng, dims, shards, -0.22, 0.18)
    return jnp.clip(spiked(values, jax.random.fold_in(rng, 3), *heavy), -reach, reach).astype(kind)


def setup_inputs(seed: int = 0) -> dict:
    seeds = jax.random.split(jax.random.key(seed), 8)
    activations = bell_draw_with(seeds[0], (TOKENS, D), TOKENS ** -0.5, 0.25, ((0, 8),), (0, 1, 8, 2.0))
    expert_ids_keys = jax.random.split(jax.random.fold_in(seeds[1], 1), TOKENS // TOK_J)
    expert_ids_turns = jax.random.permutation(jax.random.fold_in(seeds[1], 3), TOKENS // TOK_J)
    expert_ids = jax.vmap(lambda own, number: shared_out(jax.random.fold_in(seeds[1], 2), own, number, TOK_J, EXPERTS, TOP, CAP, 2))(expert_ids_keys, expert_ids_turns).reshape((TOKENS, TOP))
    gate_weights = jnp.clip(0.2 + 0.8 * jax.random.uniform(seeds[2], (TOKENS, TOP), jnp.float32) ** steps_of(seeds[2], (TOKENS, TOP), ((0, 8),), -0.2, 0.2), 0.2, 1.0)
    slot_grads = gaussian(seeds[3], (EXPERTS, SLOTS, FF), 1.0, 6.0, ((0, 8), (1, 4)))
    expert_weights = gaussian(seeds[4], (EXPERTS, D, FF), FF ** -0.5, 0.1875, ((0, 8), (1, 4)))
    shared_grads = gaussian(seeds[5], (TOKENS, FF), 1.0, 6.0, ((0, 8),))
    shared_weight = gaussian(seeds[6], (D, FF), FF ** -0.5, 0.1875, ((0, 4),))
    return dict(activations=activations, expert_ids=expert_ids, gate_weights=gate_weights, slot_grads=slot_grads, expert_weights=expert_weights, shared_grads=shared_grads, shared_weight=shared_weight)


def slot_places(block_ids):
    flattened = block_ids.reshape(-1)
    positions = jnp.arange(flattened.shape[0], dtype=jnp.int32)
    matches = (flattened[:, None] == flattened[None, :]) & (positions[None, :] < positions[:, None])
    return jnp.sum(matches.astype(jnp.int32), axis=1).reshape(block_ids.shape)


def reference(activations, expert_ids, gate_weights, slot_grads, expert_weights, shared_grads, shared_weight):
    blocks = expert_ids.reshape(N_EXPERT, TOK_J, TOP)
    places = lax.map(slot_places, blocks).reshape(TOKENS, TOP)
    source = (jnp.arange(TOKENS, dtype=jnp.int32) // TOK_J)[:, None]
    row_index = (expert_ids * SLOTS + source * CAP + places).astype(jnp.int32)

    def project(operands):
        slot_block, weight = operands
        return jnp.dot(slot_block, weight.T, preferred_element_type=jnp.float32).astype(jnp.bfloat16)

    partial_value = lax.map(project, (slot_grads, expert_weights))
    flattened = partial_value.reshape(EXPERTS * SLOTS, D)
    shared = jnp.dot(shared_grads, shared_weight.T, preferred_element_type=jnp.float32)

    def combine(operands):
        index_block, gate_block, shared_block = operands
        picked = jnp.take(flattened, index_block, axis=0).astype(jnp.float32)
        return jnp.einsum("tk,tkd->td", gate_block.astype(jnp.float32), picked) + shared_block

    combined = lax.map(combine, (row_index.reshape(N_EXPERT, TOK_J, TOP), gate_weights.reshape(N_EXPERT, TOK_J, TOP), shared.reshape(N_EXPERT, TOK_J, D)))
    combined = combined.reshape(TOKENS, D).astype(jnp.bfloat16)
    return jnp.dot(activations.T, combined, preferred_element_type=jnp.float32)
```

```python
import jax
import jax.numpy as jnp
from jax import lax
from jax.sharding import PartitionSpec as P


def source_matrix(ids, gates, first, local_experts, groups, capacity):
    tokens = ids.shape[0]
    block = tokens // groups
    experts = first + jnp.arange(local_experts, dtype=jnp.int32)
    hit = ids[:, :, None] == experts[None, None, :]
    gate = jnp.sum(jnp.where(hit, gates[:, :, None], 0.0), axis=1)
    named = jnp.any(hit, axis=1)
    ones = named.astype(jnp.bfloat16).reshape(groups, block, local_experts)
    row = jnp.arange(block, dtype=jnp.int32)
    earlier = (row[None, :] < row[:, None]).astype(jnp.bfloat16)
    place = jnp.einsum("tu,bue->bte", earlier, ones, preferred_element_type=jnp.float32)
    place = place.astype(jnp.int32).reshape(tokens, local_experts)
    source = (jnp.arange(tokens, dtype=jnp.int32) // block)[:, None]
    slot = jnp.where(named, source * capacity + place, -1)
    slots = jnp.arange(groups * capacity, dtype=jnp.int32)
    spread = jnp.where(slot[:, :, None] == slots[None, None, :], gate[:, :, None], 0.0)
    return spread.astype(jnp.bfloat16).reshape(tokens, local_experts * groups * capacity)


def on_device(
    activations, expert_ids, gate_weights, slot_grads, expert_weights, shared_grads, shared_weight
):
    local_experts, feature_block = expert_weights.shape[:2]
    groups = lax.axis_size("expert")
    slot_total = slot_grads.shape[1] * lax.axis_size("dp")
    capacity = slot_total // groups
    block, width = activations.shape
    rows = width // groups

    ids = lax.all_gather(expert_ids, "expert", axis=0, tiled=True)
    gates = lax.all_gather(gate_weights, "expert", axis=0, tiled=True)
    gathered = lax.all_gather(slot_grads, "dp", axis=1, tiled=True)
    turned = activations.T.reshape(groups, rows, block)
    columns = lax.all_to_all(turned, "expert", split_axis=0, concat_axis=0, tiled=True)
    gathered, columns, ids, gates = lax.optimization_barrier((gathered, columns, ids, gates))
    columns = columns.transpose(1, 0, 2).reshape(rows, groups * block)

    partial_value = jnp.einsum(
        "esf,edf->esd", gathered, expert_weights, preferred_element_type=jnp.float32
    ).astype(jnp.bfloat16)
    partial_value = partial_value.reshape(local_experts * slot_total, feature_block)
    first = lax.axis_index("expert") * local_experts
    spread = source_matrix(ids, gates, first, local_experts, groups, capacity)
    own = jnp.dot(spread, partial_value, preferred_element_type=jnp.float32).astype(jnp.bfloat16)
    summed = lax.psum_scatter(own, "expert", scatter_dimension=0, tiled=True)
    shared_term = jnp.einsum(
        "tf,df->td", shared_grads, shared_weight, preferred_element_type=jnp.float32
    )
    combined = (summed.astype(jnp.float32) + shared_term).astype(jnp.bfloat16)
    combined = lax.all_gather(combined, "expert", axis=0, tiled=True)
    columns, combined = lax.optimization_barrier((columns, combined))
    return jnp.dot(columns, combined, preferred_element_type=jnp.float32)


def solution(mesh):
    return jax.shard_map(
        on_device,
        mesh=mesh,
        in_specs=(
            P("expert", None),
            P("expert", None),
            P("expert", None),
            P("expert", "dp", None),
            P("expert", "dp", None),
            P("expert", None),
            P("dp", None),
        ),
        out_specs=P("expert", "dp"),
        check_vma=False,
    )
```

```python
import jax
import jax.numpy as jnp
from jax import lax
from jax.sharding import PartitionSpec as P


def source_matrix(ids, gates, first, local_experts, groups, capacity):
    tokens = ids.shape[0]
    block = tokens // groups
    experts = first + jnp.arange(local_experts, dtype=jnp.int32)
    hit = ids[:, :, None] == experts[None, None, :]
    gate = jnp.sum(jnp.where(hit, gates[:, :, None], 0.0), axis=1)
    named = jnp.any(hit, axis=1)
    ones = named.astype(jnp.bfloat16).reshape(groups, block, local_experts)
    row = jnp.arange(block, dtype=jnp.int32)
    earlier = (row[None, :] < row[:, None]).astype(jnp.bfloat16)
    place = jnp.einsum("tu,bue->bte", earlier, ones, preferred_element_type=jnp.float32)
    place = place.astype(jnp.int32).reshape(tokens, local_experts)
    source = (jnp.arange(tokens, dtype=jnp.int32) // block)[:, None]
    slot = jnp.where(named, source * capacity + place, -1)
    slots = jnp.arange(groups * capacity, dtype=jnp.int32)
    spread = jnp.where(slot[:, :, None] == slots[None, None, :], gate[:, :, None], 0.0)
    return spread.astype(jnp.bfloat16).reshape(tokens, local_experts * groups * capacity)


def on_device(
    activations, expert_ids, gate_weights, slot_grads, expert_weights, shared_grads, shared_weight
):
    local_experts, feature_block = expert_weights.shape[:2]
    groups = lax.axis_size("expert")
    slot_total = slot_grads.shape[1] * lax.axis_size("dp")
    capacity = slot_total // groups
    block, width = activations.shape
    rows = width // groups

    gathered = lax.all_gather(slot_grads, "dp", axis=1, tiled=True)
    routed = jnp.concatenate([expert_ids.astype(jnp.float32), gate_weights], axis=1)
    routed = lax.all_gather(routed, "expert", axis=0, tiled=True)
    turned = activations.T.reshape(groups, rows, block)
    turned, routed = lax.optimization_barrier((turned, routed))
    columns = lax.all_to_all(turned, "expert", split_axis=0, concat_axis=0, tiled=True)

    top = expert_ids.shape[1]
    ids, gates = routed[:, :top].astype(jnp.int32), routed[:, top:]
    first = lax.axis_index("expert") * local_experts
    spread = source_matrix(ids, gates, first, local_experts, groups, capacity)
    shared_term = jnp.einsum(
        "tf,df->td", shared_grads, shared_weight, preferred_element_type=jnp.float32
    )
    gathered, spread, shared_term = lax.optimization_barrier((gathered, spread, shared_term))

    parts = 2 if feature_block % 256 == 0 else 1
    step = feature_block // parts
    sums = []
    for part in range(parts):
        weights = expert_weights[:, part * step : (part + 1) * step]
        partial_value = jnp.einsum(
            "esf,edf->esd", gathered, weights, preferred_element_type=jnp.float32
        ).astype(jnp.bfloat16)
        partial_value = partial_value.reshape(local_experts * slot_total, step)
        own = jnp.dot(spread, partial_value, preferred_element_type=jnp.float32)
        own = own.astype(jnp.bfloat16)
        if part == 0:
            own, columns = lax.optimization_barrier((own, columns))
        sums.append(lax.psum_scatter(own, "expert", scatter_dimension=0, tiled=True))
    columns = columns.transpose(1, 0, 2).reshape(rows, groups * block)
    summed = jnp.concatenate(sums, axis=1)
    combined = (summed.astype(jnp.float32) + shared_term).astype(jnp.bfloat16)
    combined = lax.all_gather(combined, "expert", axis=0, tiled=True)
    columns, combined = lax.optimization_barrier((columns, combined))
    return jnp.dot(columns, combined, preferred_element_type=jnp.float32)


def solution(mesh):
    return jax.shard_map(
        on_device,
        mesh=mesh,
        in_specs=(
            P("expert", None),
            P("expert", None),
            P("expert", None),
            P("expert", "dp", None),
            P("expert", "dp", None),
            P("expert", None),
            P("dp", None),
        ),
        out_specs=P("expert", "dp"),
        check_vma=False,
    )
```

```python
import jax
import jax.numpy as jnp
from jax import lax
from jax.sharding import PartitionSpec as P


def source_matrix(ids, gates, first, local_experts, groups, capacity):
    tokens = ids.shape[0]
    block = tokens // groups
    experts = first + jnp.arange(local_experts, dtype=jnp.int32)
    hit = ids[:, :, None] == experts[None, None, :]
    gate = jnp.sum(jnp.where(hit, gates[:, :, None], 0.0), axis=1)
    named = jnp.any(hit, axis=1)
    ones = named.astype(jnp.bfloat16).reshape(groups, block, local_experts)
    row = jnp.arange(block, dtype=jnp.int32)
    earlier = (row[None, :] < row[:, None]).astype(jnp.bfloat16)
    place = jnp.einsum("tu,bue->bte", earlier, ones, preferred_element_type=jnp.float32)
    place = place.astype(jnp.int32).reshape(tokens, local_experts)
    source = (jnp.arange(tokens, dtype=jnp.int32) // block)[:, None]
    slot = jnp.where(named, source * capacity + place, -1)
    slots = jnp.arange(groups * capacity, dtype=jnp.int32)
    spread = jnp.where(slot[:, :, None] == slots[None, None, :], gate[:, :, None], 0.0)
    return spread.astype(jnp.bfloat16).reshape(tokens, local_experts * groups * capacity)


def on_device(
    activations, expert_ids, gate_weights, slot_grads, expert_weights, shared_grads, shared_weight
):
    local_experts, feature_block = expert_weights.shape[:2]
    groups = lax.axis_size("expert")
    slot_total = slot_grads.shape[1] * lax.axis_size("dp")
    capacity = slot_total // groups
    block, width = activations.shape
    rows = width // groups

    gathered = lax.all_gather(slot_grads, "dp", axis=1, tiled=True)
    routed = jnp.concatenate([expert_ids.astype(jnp.float32), gate_weights], axis=1)
    routed = lax.all_gather(routed, "expert", axis=0, tiled=True)
    turned = activations.T.reshape(groups, rows, block)
    turned, routed = lax.optimization_barrier((turned, routed))
    columns = lax.all_to_all(turned, "expert", split_axis=0, concat_axis=0, tiled=True)

    top = expert_ids.shape[1]
    ids, gates = routed[:, :top].astype(jnp.int32), routed[:, top:]
    first = lax.axis_index("expert") * local_experts
    spread = source_matrix(ids, gates, first, local_experts, groups, capacity)
    shared_term = jnp.einsum(
        "tf,df->td", shared_grads, shared_weight, preferred_element_type=jnp.float32
    )
    gathered, spread, shared_term = lax.optimization_barrier((gathered, spread, shared_term))

    partial_value = jnp.einsum(
        "esf,edf->esd", gathered, expert_weights, preferred_element_type=jnp.float32
    ).astype(jnp.bfloat16)
    partial_value = partial_value.reshape(local_experts * slot_total, feature_block)
    own = jnp.dot(spread, partial_value, preferred_element_type=jnp.float32)
    own, columns = lax.optimization_barrier((own.astype(jnp.bfloat16), columns))
    summed = lax.psum_scatter(own, "expert", scatter_dimension=0, tiled=True)
    columns = columns.transpose(1, 0, 2).reshape(rows, groups * block)
    combined = (summed.astype(jnp.float32) + shared_term).astype(jnp.bfloat16)
    combined = lax.all_gather(combined, "expert", axis=0, tiled=True)
    columns, combined = lax.optimization_barrier((columns, combined))
    return jnp.dot(columns, combined, preferred_element_type=jnp.float32)


def solution(mesh):
    return jax.shard_map(
        on_device,
        mesh=mesh,
        in_specs=(
            P("expert", None),
            P("expert", None),
            P("expert", None),
            P("expert", "dp", None),
            P("expert", "dp", None),
            P("expert", None),
            P("dp", None),
        ),
        out_specs=P("expert", "dp"),
        check_vma=False,
    )
```

```python
import jax
import jax.numpy as jnp
from jax import lax
from jax.sharding import PartitionSpec as P


def source_matrix(ids, gates, first, local_experts, groups, capacity, slots):
    tokens = ids.shape[0]
    block = tokens // groups
    experts = first + jnp.arange(local_experts, dtype=jnp.int32)
    hit = ids[:, :, None] == experts[None, None, :]
    gate = jnp.sum(jnp.where(hit, gates[:, :, None], 0.0), axis=1)
    named = jnp.any(hit, axis=1)
    ones = named.astype(jnp.bfloat16).reshape(groups, block, local_experts)
    row = jnp.arange(block, dtype=jnp.int32)
    earlier = (row[None, :] < row[:, None]).astype(jnp.bfloat16)
    place = jnp.einsum("tu,bue->bte", earlier, ones, preferred_element_type=jnp.float32)
    place = place.astype(jnp.int32).reshape(tokens, local_experts)
    source = (jnp.arange(tokens, dtype=jnp.int32) // block)[:, None]
    slot = jnp.where(named, source * capacity + place, -1)
    spread = jnp.where(slot[:, :, None] == slots[None, None, :], gate[:, :, None], 0.0)
    return spread.astype(jnp.bfloat16).reshape(tokens, local_experts * groups * capacity)


def on_device(
    activations, expert_ids, gate_weights, slot_grads, expert_weights, shared_grads, shared_weight
):
    local_experts, feature_block = expert_weights.shape[:2]
    groups = lax.axis_size("expert")
    slot_total = slot_grads.shape[1] * lax.axis_size("dp")
    capacity = slot_total // groups
    block, width = activations.shape
    rows = width // groups

    shard, peers = slot_grads.shape[1], lax.axis_size("dp")
    pieces = [slot_grads]
    for turn in range(1, peers):
        pairs = [(peer, peer ^ turn) for peer in range(peers)]
        pieces.append(lax.ppermute(slot_grads, "dp", pairs))
    owners = lax.axis_index("dp") ^ jnp.arange(peers, dtype=jnp.int32)
    slots = owners[:, None] * shard + jnp.arange(shard, dtype=jnp.int32)[None, :]
    slots = slots.reshape(-1)
    routed = jnp.concatenate([expert_ids.astype(jnp.float32), gate_weights], axis=1)
    routed = lax.all_gather(routed, "expert", axis=0, tiled=True)
    turned = activations.T.reshape(groups, rows, block)
    turned, routed = lax.optimization_barrier((turned, routed))
    columns = lax.all_to_all(turned, "expert", split_axis=0, concat_axis=0, tiled=True)

    top = expert_ids.shape[1]
    ids, gates = routed[:, :top].astype(jnp.int32), routed[:, top:]
    first = lax.axis_index("expert") * local_experts
    spread = source_matrix(ids, gates, first, local_experts, groups, capacity, slots)
    shared_term = jnp.einsum(
        "tf,df->td", shared_grads, shared_weight, preferred_element_type=jnp.float32
    )
    gathered = jnp.concatenate(pieces, axis=1)
    gathered, spread, shared_term = lax.optimization_barrier((gathered, spread, shared_term))

    partial_value = jnp.einsum(
        "esf,edf->esd", gathered, expert_weights, preferred_element_type=jnp.float32
    ).astype(jnp.bfloat16)
    partial_value = partial_value.reshape(local_experts * slot_total, feature_block)
    own = jnp.dot(spread, partial_value, preferred_element_type=jnp.float32)
    own, columns = lax.optimization_barrier((own.astype(jnp.bfloat16), columns))
    summed = lax.psum_scatter(own, "expert", scatter_dimension=0, tiled=True)
    columns = columns.transpose(1, 0, 2).reshape(rows, groups * block)
    combined = (summed.astype(jnp.float32) + shared_term).astype(jnp.bfloat16)
    combined = lax.all_gather(combined, "expert", axis=0, tiled=True)
    columns, combined = lax.optimization_barrier((columns, combined))
    return jnp.dot(columns, combined, preferred_element_type=jnp.float32)


def solution(mesh):
    return jax.shard_map(
        on_device,
        mesh=mesh,
        in_specs=(
            P("expert", None),
            P("expert", None),
            P("expert", None),
            P("expert", "dp", None),
            P("expert", "dp", None),
            P("expert", None),
            P("dp", None),
        ),
        out_specs=P("expert", "dp"),
        check_vma=False,
    )
```

```python
import jax
import jax.numpy as jnp
from jax import lax
from jax.sharding import PartitionSpec as P


def source_matrix(ids, gates, first, local_experts, groups, capacity, slots):
    tokens = ids.shape[0]
    block = tokens // groups
    experts = first + jnp.arange(local_experts, dtype=jnp.int32)
    hit = ids[:, :, None] == experts[None, None, :]
    gate = jnp.sum(jnp.where(hit, gates[:, :, None], 0.0), axis=1)
    named = jnp.any(hit, axis=1)
    ones = named.astype(jnp.bfloat16).reshape(groups, block, local_experts)
    row = jnp.arange(block, dtype=jnp.int32)
    earlier = (row[None, :] < row[:, None]).astype(jnp.bfloat16)
    place = jnp.einsum("tu,bue->bte", earlier, ones, preferred_element_type=jnp.float32)
    place = place.astype(jnp.int32).reshape(tokens, local_experts)
    source = (jnp.arange(tokens, dtype=jnp.int32) // block)[:, None]
    slot = jnp.where(named, source * capacity + place, -1)
    spread = jnp.where(slot[:, :, None] == slots[None, None, :], gate[:, :, None], 0.0)
    return spread.astype(jnp.bfloat16).reshape(tokens, local_experts * groups * capacity)


def on_device(
    activations, expert_ids, gate_weights, slot_grads, expert_weights, shared_grads, shared_weight
):
    local_experts, feature_block = expert_weights.shape[:2]
    groups = lax.axis_size("expert")
    slot_total = slot_grads.shape[1] * lax.axis_size("dp")
    capacity = slot_total // groups
    block, width = activations.shape
    rows = width // groups

    shard, peers = slot_grads.shape[1], lax.axis_size("dp")
    pieces = [slot_grads]
    for turn in range(1, peers):
        pairs = [(peer, peer ^ turn) for peer in range(peers)]
        pieces.append(lax.ppermute(slot_grads, "dp", pairs))
    owners = lax.axis_index("dp") ^ jnp.arange(peers, dtype=jnp.int32)
    slots = owners[:, None] * shard + jnp.arange(shard, dtype=jnp.int32)[None, :]
    slots = slots.reshape(-1)
    routed = jnp.concatenate([expert_ids.astype(jnp.float32), gate_weights], axis=1)
    routed = lax.all_gather(routed, "expert", axis=0, tiled=True)
    turned = activations.T.reshape(groups, rows, block)
    turned, routed = lax.optimization_barrier((turned, routed))
    columns = lax.all_to_all(turned, "expert", split_axis=0, concat_axis=0, tiled=True)

    top = expert_ids.shape[1]
    ids, gates = routed[:, :top].astype(jnp.int32), routed[:, top:]
    first = lax.axis_index("expert") * local_experts
    spread = source_matrix(ids, gates, first, local_experts, groups, capacity, slots)
    shared_term = jnp.einsum(
        "tf,df->td", shared_grads, shared_weight, preferred_element_type=jnp.float32
    )
    gathered = jnp.concatenate(pieces, axis=1)
    gathered, shared_term = lax.optimization_barrier((gathered, shared_term))

    partial_value = jnp.einsum(
        "esf,edf->esd", gathered, expert_weights, preferred_element_type=jnp.float32
    ).astype(jnp.bfloat16)
    partial_value = partial_value.reshape(local_experts * slot_total, feature_block)
    own = jnp.dot(spread, partial_value, preferred_element_type=jnp.float32)
    own, columns = lax.optimization_barrier((own.astype(jnp.bfloat16), columns))
    summed = lax.psum_scatter(own, "expert", scatter_dimension=0, tiled=True)
    columns = columns.transpose(1, 0, 2).reshape(rows, groups * block)
    combined = (summed.astype(jnp.float32) + shared_term).astype(jnp.bfloat16)
    combined = lax.all_gather(combined, "expert", axis=0, tiled=True)
    columns, combined = lax.optimization_barrier((columns, combined))
    return jnp.dot(columns, combined, preferred_element_type=jnp.float32)


def solution(mesh):
    return jax.shard_map(
        on_device,
        mesh=mesh,
        in_specs=(
            P("expert", None),
            P("expert", None),
            P("expert", None),
            P("expert", "dp", None),
            P("expert", "dp", None),
            P("expert", None),
            P("dp", None),
        ),
        out_specs=P("expert", "dp"),
        check_vma=False,
    )
```
